512 devices in a mesh: seq: 32 (over z_hi, y, core), rep: 4 (over z_lo), tensor: 4 (over x).
Axes of the slice: x: 4, y: 4, z: 16 (z_hi: 4, z_lo: 4; z = z_hi * 4 + z_lo), core: 2. Of those that a mesh axis runs over, the one named last changes fastest.
Arguments:
- key_value_rows: bfloat16 [4, 49152, 8, 256], P('rep', ('seq', 'tensor')), may hold values from -32 to 32
- queries: bfloat16 [4, 64, 64, 128], P('rep', None, 'tensor'), may hold values from -136 to 136
- w_comp: bfloat16 [2048, 512], replicated, may hold values from -0.125 to 0.125
- latent_gain: bfloat16 [512], replicated, may hold values from 0.099609375 to 1.8984375
- w_up: bfloat16 [8, 512, 256], P('tensor'), may hold values from -0.25 to 0.25
- w_out: bfloat16 [8192, 8192], P('tensor', 'seq'), may hold values from -0.0625 to 0.0625
- replica_order: int32 [4], replicated, may hold values from 0 to 3, each once
Outputs:
- decoded: bfloat16 [4, 64, 8192], P('rep', None, 'seq')
The draws below stay inside these ranges and needn't reach their ends.
Inputs may be any that keep to these rules, and one draw needn't show every extreme that they name: replica_order is a permutation of the prompts.
All inputs are finite; a program needn't handle non-finite values.
Results may differ from the reference program's by a relative error of at most 0.01.
Values may be sent and summed in bfloat16 or wider, within the bound.
A program may use at most 64 MiB of HBM per device.

```python
import math
import jax
import jax.numpy as jnp
from jax import lax

D = 8192
HEADS = 64
GROUPS = 8
HD = 128
LAT = 512
NEW = 64
PROMPTS = 4
TOKENS = 49152


def scaled_rows(key, base):
    k_row, k_col = jax.random.split(key, 2)
    shape = base.shape
    row_scale = jnp.exp(jax.random.uniform(k_row, shape[:3] + (1,), jnp.float32, 0.0, math.log(10.0)))
    col_scale = jnp.exp(jax.random.uniform(k_col, (1, 1) + shape[2:], jnp.float32, 0.0, math.log(10.0)))
    return jnp.clip(base * row_scale * col_scale / 10.0, -32.0, 32.0)


def draw_key_value_rows(key, part):
    key = jax.random.fold_in(key, 11)
    k_base = jax.random.fold_in(key, 0)
    k_scale = jax.random.fold_in(key, 2)
    shape = (PROMPTS, TOKENS, GROUPS, 2 * HD)
    base = jax.random.normal(k_base, shape, jnp.float32)
    return scaled_rows(k_scale, base).astype(jnp.bfloat16)


def draw_queries(key, part):
    key = jax.random.fold_in(key, 23)
    k_base = jax.random.fold_in(key, 0)
    shape = (PROMPTS, NEW, HEADS, HD)
    base = jax.random.normal(k_base, shape, jnp.float32)
    return base.astype(jnp.bfloat16)


def shard_levels(rng, shape, cuts, least, top_value):
    loudness = 1.0
    for dim, parts in cuts:
        draws = jax.random.uniform(jax.random.fold_in(jax.random.fold_in(rng, 6), dim), (parts,), jnp.float32, least / len(cuts), top_value / len(cuts))
        loudness = loudness * jnp.repeat(jnp.exp(draws), shape[dim] // parts).reshape((-1,) + (1,) * (len(shape) - 1 - dim))
    return loudness


def scatter_about(key, extent, width, most, cuts=(), held_as=jnp.bfloat16):
    values = jax.random.normal(key, extent, jnp.float32) * width
    if len(cuts) > 0:
        values = shard_levels(key, extent, cuts, -0.22, 0.18) * values
    return jnp.clip(values, min=-most, max=most).astype(held_as)


def setup_inputs(seed: int = 0) -> dict:
    seeds = jax.random.split(jax.random.key(seed), 8)
    return {
        "key_value_rows": draw_key_value_rows(jax.random.fold_in(seeds[7], 71), 0),
        "queries": draw_queries(jax.random.fold_in(seeds[7], 71), 0),
        "w_comp": scatter_about(seeds[2], (GROUPS * 2 * HD, LAT), (GROUPS * 2 * HD) ** -0.5, 0.125),
        "latent_gain": jnp.clip(1.0 + 0.18 * jax.random.normal(seeds[3], (LAT,), jnp.float32), 0.099609375, 1.8984375).astype(jnp.bfloat16),
        "w_up": scatter_about(seeds[4], (GROUPS, LAT, 2 * HD), LAT ** -0.5, 0.25, ((0, 4),)),
        "w_out": scatter_about(seeds[5], (HEADS * HD, D), (HEADS * HD) ** -0.5, 0.0625, ((0, 4), (1, 32))),
        "replica_order": jax.random.permutation(seeds[6], PROMPTS).astype(jnp.int32),
    }


def compress(rows, weight, gain):
    projected = jnp.dot(rows, weight, preferred_element_type=jnp.float32)
    scale = lax.rsqrt(lax.optimization_barrier(jnp.mean(projected * projected, axis=-1, keepdims=True)) + 1e-06)
    return (projected * scale * gain.astype(jnp.float32)).astype(jnp.bfloat16)

def attend_group(latent_state, operands):
    query, lift = operands
    lifted = jnp.dot(latent_state, lift, preferred_element_type=jnp.float32).astype(jnp.bfloat16)
    head_size = query.shape[-1]
    keys = lifted[:, :head_size]
    values = lifted[:, head_size:]
    scores = jnp.einsum('nhd,td->nht', query.astype(jnp.float32), keys.astype(jnp.float32)) * head_size ** (-0.5)
    top = lax.optimization_barrier(jnp.max(scores, axis=-1, keepdims=True))
    expo = jnp.exp(scores - top)
    total = lax.optimization_barrier(jnp.sum(expo, axis=-1))
    weights = lax.optimization_barrier(expo.astype(jnp.bfloat16))
    summed = jnp.einsum('nht,td->nhd', weights.astype(jnp.float32), values.astype(jnp.float32))
    return (summed / total[..., None]).astype(jnp.bfloat16)

def reference(key_value_rows, queries, w_comp, latent_gain, w_up, w_out, replica_order):
    groups = w_up.shape[0]
    new_count = queries.shape[1]
    heads = queries.shape[2]
    head_size = queries.shape[3]
    outputs = []
    for replica in range(queries.shape[0]):
        prompt = replica_order[replica]
        rows = key_value_rows[prompt]
        rows = rows.reshape(rows.shape[0], -1)
        latent_state = compress(rows, w_comp, latent_gain)
        query = queries[replica].reshape(new_count, groups, heads // groups, head_size)
        query = jnp.moveaxis(query, 1, 0)
        attended_values = lax.map(partial_group(latent_state), (query, w_up))
        attended_values = jnp.moveaxis(attended_values, 0, 1).reshape(new_count, heads * head_size)
        outputs.append(jnp.dot(attended_values, w_out, preferred_element_type=jnp.float32).astype(jnp.bfloat16))
    return jnp.stack(outputs)

def partial_group(latent_state):

    def inner(operands):
        return attend_group(latent_state, operands)
    return inner
```

```python
import functools
import math

import jax
import jax.numpy as jnp
from jax import lax
from jax.experimental import pallas as pl
from jax.experimental.pallas import tpu as pltpu
from jax.sharding import PartitionSpec as P

MESH = pl.DeviceIdType.MESH
F32 = jnp.float32
BF16 = jnp.bfloat16

TOK = 384
CH = 96
NCH = TOK // CH
HEADS = 16
NEW = 64
HD = 128
LAT = 512
COLS = 8 * NEW
C2 = math.log2(math.e) / math.sqrt(HD)


def dev(zhi, y, core, zlo, x):
    return (zhi * 8 + y * 2 + core, zlo, x)


def three(row):
    hi = row.astype(BF16).astype(F32)
    mid = (row - hi).astype(BF16).astype(F32)
    low = row - hi - mid
    zero = jnp.zeros((13, row.shape[1]), F32)
    return jnp.concatenate([hi, mid, low, zero], axis=0).astype(BF16)


def merge(parts):
    top = functools.reduce(jnp.maximum, [t for _, t in parts])
    scale = [jnp.exp2(t - top) for _, t in parts]
    total = functools.reduce(jnp.add, scale)
    inv = 1.0 / total
    value = functools.reduce(jnp.add, [v * (s * inv) for (v, _), s in zip(parts, scale)])
    return value, top + jnp.log2(total)


def unpack(ref, rows):
    value = ref[:rows].astype(F32)
    tail = ref[rows:].astype(F32)
    return value, tail[0:1] + tail[1:2] + tail[2:3]


def kernel(
    kv_hbm, q_hbm, wc_hbm, gain_ref, wup_hbm, wout_hbm, order_ref, out_ref,
    kv, kvf, wc, wup, wout, lat, qbuf, qf, qt, m_ref, l_ref, o_ref,
    send1, recv1, send2, recv2, zbuf, ycbuf, xbuf, zstage,
    kv_sem, w_sem, lat_ss, lat_rs, q_ss, q_rs, s1, r1, s2, r2, s3, r3, s4, r4, s5, r5,
):
    seq = lax.axis_index("seq")
    zlo = lax.axis_index("rep")
    x = lax.axis_index("tensor")
    zhi = seq // 8
    yc = seq % 8
    y = yc // 2
    core = yc % 2
    z = zhi * 4 + zlo

    def at_x(step):
        return (seq, zlo, (x + step) % 4)

    def at_z(step):
        there = (z + step) % 16
        return ((there // 4) * 8 + yc, there % 4, x)

    def at_yc(step):
        return (zhi * 8 + (yc + step) % 8, zlo, x)

    barrier = pltpu.get_barrier_semaphore()
    peers = [at_x(k) for k in range(1, 4)] + [at_z(k) for k in range(1, 16)] + [at_yc(k) for k in range(1, 8)]
    for peer in peers:
        pl.semaphore_signal(barrier, inc=1, device_id=peer, device_id_type=MESH)

    kv_in = [pltpu.make_async_copy(kv_hbm.at[pl.ds(c * CH, CH)], kv.at[c], kv_sem.at[c]) for c in range(NCH)]
    wc_in = pltpu.make_async_copy(wc_hbm, wc, w_sem.at[0])
    wup_in = pltpu.make_async_copy(wup_hbm, wup, w_sem.at[1])
    wout_in = pltpu.make_async_copy(wout_hbm, wout, w_sem.at[2])
    q_in = pltpu.make_async_copy(q_hbm, qbuf.at[0], w_sem.at[3])
    kv_in[0].start()
    wc_in.start()
    for c in range(1, NCH):
        kv_in[c].start()
    wup_in.start()
    q_in.start()
    wout_in.start()

    pl.semaphore_wait(barrier, len(peers))

    q_copies = []
    for n, (step, slot) in enumerate(((1, 3), (-1, 1))):
        q_copies.append(pltpu.make_async_remote_copy(
            src_ref=q_hbm, dst_ref=qbuf.at[slot], send_sem=q_ss.at[n], recv_sem=q_rs.at[n],
            device_id=at_z(step), device_id_type=MESH))
    for copy in q_copies:
        copy.start()

    def own_copy(c, way):
        return pltpu.make_async_remote_copy(
            src_ref=lat.at[c // 2, c % 2],
            dst_ref=lat.at[2 + way + 2 * (c // 2), c % 2],
            send_sem=lat_ss.at[4 * way + c],
            recv_sem=lat_rs.at[4 * way + c],
            device_id=at_x(1 if way == 0 else -1),
            device_id_type=MESH,
        )

    def pass_on(c):
        way = 0 if c < 2 else 1
        return pltpu.make_async_remote_copy(
            src_ref=lat.at[2 + way + 2 * (c // 2), c % 2],
            dst_ref=lat.at[6 + c // 2, c % 2],
            send_sem=lat_ss.at[8 + c],
            recv_sem=lat_rs.at[8 + c],
            device_id=at_x(1 if way == 0 else -1),
            device_id_type=MESH,
        )

    wc_in.wait()

    def compress(c, carry):
        pltpu.make_async_copy(kv_hbm.at[pl.ds(c * CH, CH)], kv.at[c], kv_sem.at[c]).wait()
        wide = kv[c].astype(F32).reshape(CH * 8, 2 * HD)
        for part in range(2):
            kvf[part] = wide[:, part * HD:(part + 1) * HD]
        rows = jnp.concatenate(
            [kvf[part, pl.ds(g, CH, stride=8), :].astype(BF16) for g in range(8) for part in range(2)], axis=1)
        projected = jnp.dot(rows, wc[...], preferred_element_type=F32)
        scale = lax.rsqrt(jnp.mean(projected * projected, axis=-1, keepdims=True) + 1e-06)
        lat[c // 2, c % 2] = (projected * scale * gain_ref[...].astype(F32)).astype(BF16)
        own_copy(c, 0).start()
        own_copy(c, 1).start()
        return carry

    lax.fori_loop(0, NCH, compress, 0)

    for c in (0, 1):
        own_copy(c, 0).wait_recv()
        pass_on(c).start()

    q_pass = []
    for n, (slot, step) in enumerate(((3, 1), (1, -1))):
        q_copies[n].wait_recv()
        half = pl.ds(n * (NEW // 2), NEW // 2)
        copy = pltpu.make_async_remote_copy(
            src_ref=qbuf.at[slot, half], dst_ref=qbuf.at[2, half],
            send_sem=q_ss.at[2 + n], recv_sem=q_rs.at[2 + n],
            device_id=at_z(step), device_id_type=MESH)
        copy.start()
        q_pass.append(copy)

    for c in (2, 3):
        own_copy(c, 1).wait_recv()
        pass_on(c).start()

    q_in.wait()
    for copy in q_pass:
        copy.wait_recv()

    source = jnp.int32(0)
    for r in range(4):
        source = source + jnp.where(order_ref[r] == zlo, r, 0)
    pick = (source - zlo + 4) % 4
    qf[...] = qbuf[pick].astype(F32).reshape(NEW * HEADS, HD)
    for pair in range(HEADS // 2):
        two = jnp.concatenate(
            [qf[pl.ds(2 * pair + h, NEW, stride=HEADS), :] for h in range(2)], axis=0)
        qt[pair // 4, :, (pair % 4) * 128:(pair % 4 + 1) * 128] = two.T.astype(BF16)

    wup_in.wait()
    m_ref[...] = jnp.full(m_ref.shape, -1e30, F32)
    l_ref[...] = jnp.zeros(l_ref.shape, F32)
    o_ref[...] = jnp.zeros(o_ref.shape, F32)

    def attend(i, carry):
        @pl.when(i == 3)
        def _():
            own_copy(0, 1).wait_recv()
            own_copy(1, 1).wait_recv()

        @pl.when(i == 4)
        def _():
            own_copy(2, 0).wait_recv()
            own_copy(3, 0).wait_recv()

        @pl.when(i == 6)
        def _():
            pass_on(0).wait_recv()
            pass_on(1).wait_recv()

        @pl.when(i == 7)
        def _():
            pass_on(2).wait_recv()
            pass_on(3).wait_recv()

        state = lat[i].reshape(2 * CH, LAT)
        for g in range(2):
            lifted = jnp.dot(state, wup[g], preferred_element_type=F32).astype(BF16)
            keys = lifted[:, :HD]
            values = lifted[:, HD:]
            scores = jnp.dot(keys, qt[g], preferred_element_type=F32)
            old = m_ref[g]
            top = jnp.maximum(old, jnp.max(scores, axis=0, keepdims=True))
            expo = jnp.exp2((scores - top) * C2)
            fade = jnp.exp2((old - top) * C2)
            l_ref[g] = l_ref[g] * fade + jnp.sum(expo, axis=0, keepdims=True)
            m_ref[g] = top
            o_ref[g] = o_ref[g] * fade + lax.dot_general(
                values, expo.astype(BF16), (((0,), (0,)), ((), ())), preferred_element_type=F32)
        return carry

    lax.fori_loop(0, 8, attend, 0)

    for g in range(2):
        total = l_ref[g]
        value = o_ref[g] * (1.0 / total)
        tail = three(m_ref[g] * C2 + jnp.log2(total))
        for k in range(4):
            cols = slice(128 * k, 128 * (k + 1))
            send1[4 * g + k, :HD] = value[:, cols].astype(BF16)
            send1[4 * g + k, HD:] = tail[:, cols]

    def scatter1(k):
        return pltpu.make_async_remote_copy(
            src_ref=send1.at[(yc + k) % 8], dst_ref=recv1.at[k - 1],
            send_sem=s1.at[k - 1], recv_sem=r1.at[k - 1],
            device_id=at_yc(k), device_id_type=MESH)

    for k in range(1, 8):
        scatter1(k).start()
    parts = [unpack(send1.at[yc], HD)]
    for k in range(1, 8):
        scatter1(k).wait_recv()
        parts.append(unpack(recv1.at[k - 1], HD))
    value, level = merge(parts)

    tail = three(level)
    for k in range(4):
        send2[k, :32] = value[32 * k:32 * (k + 1)].astype(BF16)
        send2[k, 32:] = tail

    def scatter2(k):
        return pltpu.make_async_remote_copy(
            src_ref=send2.at[(zhi + k) % 4], dst_ref=recv2.at[k - 1],
            send_sem=s2.at[k - 1], recv_sem=r2.at[k - 1],
            device_id=at_z(4 * k), device_id_type=MESH)

    for k in range(1, 4):
        scatter2(k).start()
    parts = [unpack(send2.at[zhi], 32)]
    for k in range(1, 4):
        scatter2(k).wait_recv()
        parts.append(unpack(recv2.at[k - 1], 32))
    value, _ = merge(parts)

    zstage[...] = value.astype(BF16)
    zbuf[z] = value.astype(BF16)

    def spread_z(k):
        return pltpu.make_async_remote_copy(
            src_ref=zstage, dst_ref=zbuf.at[z],
            send_sem=s3.at[k - 1], recv_sem=r3.at[k - 1],
            device_id=at_z(k), device_id_type=MESH)

    for k in range(1, 16):
        spread_z(k).start()
    for k in range(1, 16):
        spread_z(k).wait_recv()

    wanted = order_ref[zlo]
    mine = jnp.concatenate([zbuf[4 * q + wanted] for q in range(4)], axis=0)
    ycbuf[yc] = mine

    def spread_yc(k):
        return pltpu.make_async_remote_copy(
            src_ref=ycbuf.at[yc], dst_ref=ycbuf.at[yc],
            send_sem=s4.at[k - 1], recv_sem=r4.at[k - 1],
            device_id=at_yc(k), device_id_type=MESH)

    for k in range(1, 8):
        spread_yc(k).start()
    for k in range(1, 8):
        spread_yc(k).wait_recv()

    wout_in.wait()
    rows = []
    for j in range(8):
        part = ycbuf[j].astype(F32).T.astype(BF16)
        rows += [part[:NEW], part[NEW:]]
    partial = jnp.dot(jnp.concatenate(rows, axis=1), wout[...], preferred_element_type=F32)

    xbuf[0] = partial.astype(BF16)

    def spread_x(k):
        return pltpu.make_async_remote_copy(
            src_ref=xbuf.at[0], dst_ref=xbuf.at[k],
            send_sem=s5.at[k - 1], recv_sem=r5.at[k - 1],
            device_id=at_x(k), device_id_type=MESH)

    for k in range(1, 4):
        spread_x(k).start()
    for k in range(1, 4):
        spread_x(k).wait_recv()
        partial = partial + xbuf[k].astype(F32)
    out_ref[0] = partial.astype(BF16)

    for c in range(NCH):
        own_copy(c, 0).wait_send()
        own_copy(c, 1).wait_send()
        pass_on(c).wait_send()
    for copy in q_copies + q_pass:
        copy.wait_send()
    for k in range(1, 8):
        scatter1(k).wait_send()
        spread_yc(k).wait_send()
    for k in range(1, 4):
        scatter2(k).wait_send()
        spread_x(k).wait_send()
    for k in range(1, 16):
        spread_z(k).wait_send()


def shards(key_value_rows, queries, w_comp, latent_gain, w_up, w_out, replica_order):
    dma = lambda n: pltpu.SemaphoreType.DMA((n,))
    anywhere = pl.BlockSpec(memory_space=pl.ANY)
    vmem = pl.BlockSpec(memory_space=pltpu.VMEM)
    smem = pl.BlockSpec(memory_space=pltpu.SMEM)
    return pl.pallas_call(
        kernel,
        out_shape=jax.ShapeDtypeStruct((1, NEW, 256), BF16),
        in_specs=[anywhere, anywhere, anywhere, vmem, anywhere, anywhere, smem],
        out_specs=vmem,
        scratch_shapes=[
            pltpu.VMEM((NCH, CH, 8, 2 * HD), BF16),
            pltpu.VMEM((2, CH * 8, HD), F32),
            pltpu.VMEM((2048, LAT), BF16),
            pltpu.VMEM((2, LAT, 2 * HD), BF16),
            pltpu.VMEM((2048, 256), BF16),
            pltpu.VMEM((8, 2, CH, LAT), BF16),
            pltpu.VMEM((4, NEW, HEADS, HD), BF16),
            pltpu.VMEM((NEW * HEADS, HD), F32),
            pltpu.VMEM((2, HD, COLS), BF16),
            pltpu.VMEM((2, 1, COLS), F32),
            pltpu.VMEM((2, 1, COLS), F32),
            pltpu.VMEM((2, HD, COLS), F32),
            pltpu.VMEM((8, HD + 16, 128), BF16),
            pltpu.VMEM((7, HD + 16, 128), BF16),
            pltpu.VMEM((4, 48, 128), BF16),
            pltpu.VMEM((3, 48, 128), BF16),
            pltpu.VMEM((16, 32, 128), BF16),
            pltpu.VMEM((8, HD, 128), BF16),
            pltpu.VMEM((4, NEW, 256), BF16),
            pltpu.VMEM((32, 128), BF16),
            dma(NCH), dma(4), dma(12), dma(12), dma(4), dma(4),
            dma(7), dma(7), dma(3), dma(3), dma(15), dma(15), dma(7), dma(7), dma(3), dma(3),
        ],
        compiler_params=pltpu.CompilerParams(
            collective_id=0, has_side_effects=True, vmem_limit_bytes=63 * 1024 * 1024),
        cost_estimate=pl.CostEstimate(flops=3_000_000_000, bytes_accessed=7_000_000, transcendentals=1_600_000),
    )(key_value_rows[0], queries[0], w_comp, latent_gain.reshape(1, LAT), w_up, w_out, replica_order)


def solution(mesh):
    placed = (
        P("rep", ("seq", "tensor"), None, None),
        P("rep", None, "tensor", None),
        P(),
        P(),
        P("tensor", None, None),
        P("tensor", "seq"),
        P(),
    )
    return jax.shard_map(
        shards, mesh=mesh, in_specs=placed, out_specs=P("rep", None, "seq"), check_vma=False
    )
```

```python
import functools
import math

import jax
import jax.numpy as jnp
from jax import lax
from jax.experimental import pallas as pl
from jax.experimental.pallas import tpu as pltpu
from jax.sharding import PartitionSpec as P

MESH = pl.DeviceIdType.MESH
F32 = jnp.float32
BF16 = jnp.bfloat16

TOK = 384
CH = 96
NCH = TOK // CH
NEW = 64
HD = 128
LAT = 512
COLS = 8 * NEW
C2 = math.log2(math.e) / math.sqrt(HD)


def three(row):
    hi = row.astype(BF16).astype(F32)
    mid = (row - hi).astype(BF16).astype(F32)
    low = row - hi - mid
    zero = jnp.zeros((13, row.shape[1]), F32)
    return jnp.concatenate([hi, mid, low, zero], axis=0).astype(BF16)


def merge(parts):
    top = functools.reduce(jnp.maximum, [t for _, t in parts])
    scale = [jnp.exp2(t - top) for _, t in parts]
    total = functools.reduce(jnp.add, scale)
    inv = 1.0 / total
    value = functools.reduce(jnp.add, [v * (s * inv) for (v, _), s in zip(parts, scale)])
    return value, top + jnp.log2(total)


def unpack(ref, rows):
    value = ref[:rows].astype(F32)
    tail = ref[rows:].astype(F32)
    return value, tail[0:1] + tail[1:2] + tail[2:3]


def kernel(
    kv_hbm, q_hbm, wc_hbm, gain_ref, wup_hbm, wout_hbm, order_ref, out_ref,
    kv, kvf, wc, wup, wout, lat, qbuf, qf, qt, m_ref, l_ref, o_ref,
    send1, recv1, send2, recv2, heads, xbuf, zbuf,
    kv_sem, w_sem, lat_ss, lat_rs, sib_ss, sib_rs, q_ss, q_rs, s1, r1, s2, r2, s3, r3, s4, r4, s5, r5, far,
):
    seq = lax.axis_index("seq")
    zlo = lax.axis_index("rep")
    x = lax.axis_index("tensor")
    zhi = seq // 8
    y = seq % 8 // 2
    core = seq % 2
    z = zhi * 4 + zlo

    def at_x(step):
        return (seq, zlo, (x + step + 4) % 4)

    def at_y(step):
        return (zhi * 8 + (y + step) % 4 * 2 + core, zlo, x)

    def at_z(step):
        there = (z + step + 16) % 16
        return (there // 4 * 8 + y * 2 + core, there % 4, x)

    def at_zlo(step):
        return (seq, (zlo + step) % 4, x)

    sibling = (zhi * 8 + y * 2 + 1 - core, zlo, x)

    def copy_to(device, src, dst, send_sem, recv_sem):
        return pltpu.make_async_remote_copy(
            src_ref=src, dst_ref=dst, send_sem=send_sem, recv_sem=recv_sem,
            device_id=device, device_id_type=MESH)

    barrier = pltpu.get_barrier_semaphore()
    near = [sibling] + [at_x(k) for k in (1, 2, 3)] + [at_y(k) for k in (1, 2, 3)]
    near += [at_zlo(k) for k in (1, 2, 3)] + [at_z(k) for k in (1, -1)]
    for peer in near:
        pl.semaphore_signal(barrier, inc=1, device_id=peer, device_id_type=MESH)

    kv_in = [pltpu.make_async_copy(kv_hbm.at[pl.ds(c * CH, CH)], kv.at[c], kv_sem.at[c]) for c in range(NCH)]
    wc_in = pltpu.make_async_copy(wc_hbm, wc, w_sem.at[0])
    wup_in = pltpu.make_async_copy(wup_hbm.at[core], wup, w_sem.at[1])
    wout_in = pltpu.make_async_copy(wout_hbm, wout, w_sem.at[2])
    q_here = q_hbm.at[:, pl.ds(core * 8, 8)]
    q_in = pltpu.make_async_copy(q_here, qbuf.at[0], w_sem.at[3])
    kv_in[0].start()
    wc_in.start()
    for c in range(1, NCH):
        kv_in[c].start()
    q_in.start()
    wup_in.start()
    wout_in.start()

    pl.semaphore_wait(barrier, len(near))

    def tell(n, step):
        for way in (1, -1):
            pl.semaphore_signal(far.at[n], inc=1, device_id=at_z(way * step), device_id_type=MESH)

    tell(0, 1)

    def half(n):
        return pl.ds(n * (NEW // 2), NEW // 2)

    def q_send(way, n):
        slot = (3, 1)[way]
        return copy_to(
            at_z((1, -1)[way]), q_hbm.at[half(n), pl.ds(core * 8, 8)], qbuf.at[slot, half(n)],
            q_ss.at[2 * way + n], q_rs.at[2 * way + n])

    def q_pass(way):
        return copy_to(
            at_z((1, -1)[way]), qbuf.at[(3, 1)[way], half(way)], qbuf.at[2, half(way)],
            q_ss.at[4 + way], q_rs.at[4 + way])

    for n in range(2):
        q_send(0, n).start()
        q_send(1, 1 - n).start()
    sent = [q_send(way, n) for way in range(2) for n in range(2)]

    def first(c):
        return copy_to(
            at_x(1 - 2 * (c % 2)), lat.at[c, core], lat.at[4 + c, core], lat_ss.at[c], lat_rs.at[4 + c])

    def second(c):
        there = 9 + c - 2 * (c % 2)
        return copy_to(
            at_x(2 * (c % 2) - 1), lat.at[c, core], lat.at[there, core], lat_ss.at[4 + c], lat_rs.at[there])

    def pass_on(s):
        return copy_to(
            at_x(1 - 2 * (s % 2)), lat.at[s, core], lat.at[s + 8, core], lat_ss.at[4 + s], lat_rs.at[s + 8])

    def share(s):
        return copy_to(sibling, lat.at[s, core], lat.at[s, core], sib_ss.at[s], sib_rs.at[s])

    def arrive(s):
        copy_to(sibling, lat.at[s, core], lat.at[s, core], sib_ss.at[s], lat_rs.at[s]).wait_recv()

    wc_in.wait()

    def compress(c, carry):
        pltpu.make_async_copy(kv_hbm.at[pl.ds(c * CH, CH)], kv.at[c], kv_sem.at[c]).wait()
        wide = kv[c].astype(F32).reshape(CH * 8, 2 * HD)
        for part in range(2):
            kvf[part] = wide[:, part * HD:(part + 1) * HD]
        rows = jnp.concatenate(
            [kvf[part, pl.ds(g, CH, stride=8), :].astype(BF16) for g in range(8) for part in range(2)], axis=1)
        projected = jnp.dot(rows, wc[...], preferred_element_type=F32)
        scale = lax.rsqrt(jnp.mean(projected * projected, axis=-1, keepdims=True) + 1e-06)
        gain = gain_ref[...].astype(F32).reshape(1, LAT)
        lat[c, core] = (projected * scale * gain).astype(BF16)
        first(c).start()
        share(c).start()
        return carry

    lax.fori_loop(0, NCH, compress, 0)
    for c in (1, 0, 3, 2):
        second(c).start()
    sent += [first(c) for c in range(4)] + [second(c) for c in range(4)]

    pl.semaphore_wait(far.at[0], 2)
    tell(1, 2)
    for way in range(2):
        q_send(way, way).wait_recv()
        q_pass(way).start()
    sent += [q_pass(way) for way in range(2)]

    def relay(s, carry):
        arrive(s)
        pass_on(s).start()
        share(s).start()
        return carry

    lax.fori_loop(4, 8, relay, 0)
    sent += [pass_on(s) for s in range(4, 8)] + [share(s) for s in range(16)]

    pl.semaphore_wait(far.at[1], 2)
    tell(2, 4)
    q_in.wait()
    for way in range(2):
        q_send(way, 1 - way).wait_recv()
    for way in range(2):
        q_pass(way).wait_recv()

    source = jnp.int32(0)
    for r in range(4):
        source = source + jnp.where(order_ref[r] == zlo, r, 0)
    pick = (source - zlo + 4) % 4
    qf[...] = qbuf[pick].astype(F32).reshape(NEW * 8, HD)
    for pair in range(4):
        two = jnp.concatenate([qf[pl.ds(2 * pair + h, NEW, stride=8), :] for h in range(2)], axis=0)
        qt[:, pair * 128:(pair + 1) * 128] = two.T.astype(BF16)

    wup_in.wait()
    m_ref[...] = jnp.full(m_ref.shape, -1e30, F32)
    l_ref[...] = jnp.zeros(l_ref.shape, F32)
    o_ref[...] = jnp.zeros(o_ref.shape, F32)

    def attend(s, carry):
        for now, coming in ((4, 8), (5, 9), (6, 10), (7, 11), (10, 12), (11, 13), (13, 14), (14, 15)):
            @pl.when(s == now)
            def _():
                arrive(coming)
                share(coming).start()

        share(s).wait_recv()
        lifted = jnp.dot(
            lat[s].reshape(2 * CH, LAT), wup[...], preferred_element_type=F32).astype(BF16)
        keys = lifted[:, :HD]
        values = lifted[:, HD:]
        scores = jnp.dot(keys, qt[...], preferred_element_type=F32)
        old = m_ref[...]
        top = jnp.maximum(old, jnp.max(scores, axis=0, keepdims=True))
        expo = jnp.exp2((scores - top) * C2)
        fade = jnp.exp2((old - top) * C2)
        l_ref[...] = l_ref[...] * fade + jnp.sum(expo, axis=0, keepdims=True)
        m_ref[...] = top
        o_ref[...] = o_ref[...] * fade + lax.dot_general(
            values, expo.astype(BF16), (((0,), (0,)), ((), ())), preferred_element_type=F32)
        return carry

    lax.fori_loop(0, 16, attend, 0)

    total = l_ref[...]
    value = o_ref[...] * (1.0 / total)
    tail = three(m_ref[...] * C2 + jnp.log2(total))
    for k in range(4):
        cols = slice(128 * k, 128 * (k + 1))
        send1[k, :HD] = value[:, cols].astype(BF16)
        send1[k, HD:] = tail[:, cols]

    def scatter(k):
        return copy_to(at_y(k), send1.at[(y + k) % 4], recv1.at[k - 1], s1.at[k - 1], r1.at[k - 1])

    for k in (2, 1, 3):
        scatter(k).start()
    sent += [scatter(k) for k in (1, 2, 3)]
    parts = [unpack(send1.at[y], HD)]
    for k in (1, 3, 2):
        scatter(k).wait_recv()
        parts.append(unpack(recv1.at[k - 1], HD))
    value, level = merge(parts)

    send2[:HD] = value.astype(BF16)
    send2[HD:] = three(level)
    pl.semaphore_wait(far.at[2], 2)

    def across(k):
        return copy_to(at_z(4 * k), send2, recv2.at[k - 1], s2.at[k - 1], r2.at[k - 1])

    for k in (2, 1, 3):
        across(k).start()
    sent += [across(k) for k in (1, 2, 3)]
    parts = [unpack(send2, HD)]
    for k in (1, 3, 2):
        across(k).wait_recv()
        parts.append(unpack(recv2.at[k - 1], HD))
    value, _ = merge(parts)

    heads[core, y] = value.T.astype(BF16)

    def spread(k):
        return copy_to(at_y(k), heads.at[core, y], heads.at[core, y], s3.at[k], r3.at[k])

    def pair(k):
        there = heads.at[core, (y - k + 4) % 4]
        return copy_to(sibling, there, there, s3.at[4 + k], r3.at[4 + k])

    for k in (2, 1, 3):
        spread(k).start()
    pair(0).start()
    for k in (1, 3, 2):
        spread(k).wait_recv()
        pair(k).start()
    for k in range(4):
        pair(k).wait_recv()
    sent += [spread(k) for k in (1, 2, 3)] + [pair(k) for k in range(4)]

    wout_in.wait()
    rows = [heads[g, k, h * NEW:(h + 1) * NEW] for g in range(2) for k in range(4) for h in range(2)]
    partial = jnp.dot(jnp.concatenate(rows, axis=1), wout[...], preferred_element_type=F32)

    xbuf[0] = partial.astype(BF16)

    def add_x(k):
        return copy_to(at_x(k), xbuf.at[0], xbuf.at[k], s4.at[k - 1], r4.at[k - 1])

    for k in (2, 1, 3):
        add_x(k).start()
    sent += [add_x(k) for k in (1, 2, 3)]
    for k in (1, 3, 2):
        add_x(k).wait_recv()
        partial = partial + xbuf[k].astype(F32)

    zbuf[0] = partial.astype(BF16)

    def reply(k):
        return copy_to(at_zlo(k), zbuf.at[0], zbuf.at[k], s5.at[k - 1], r5.at[k - 1])

    for k in (2, 1, 3):
        reply(k).start()
    sent += [reply(k) for k in (1, 2, 3)]
    for k in (1, 3, 2):
        reply(k).wait_recv()
    out_ref[0] = zbuf[(zlo - order_ref[zlo] + 4) % 4]

    for copy in sent:
        copy.wait_send()


def shards(key_value_rows, queries, w_comp, latent_gain, w_up, w_out, replica_order):
    dma = lambda n: pltpu.SemaphoreType.DMA((n,))
    anywhere = pl.BlockSpec(memory_space=pl.ANY)
    vmem = pl.BlockSpec(memory_space=pltpu.VMEM)
    smem = pl.BlockSpec(memory_space=pltpu.SMEM)
    return pl.pallas_call(
        kernel,
        out_shape=jax.ShapeDtypeStruct((1, NEW, 256), BF16),
        in_specs=[anywhere, anywhere, anywhere, vmem, anywhere, anywhere, smem],
        out_specs=vmem,
        scratch_shapes=[
            pltpu.VMEM((NCH, CH, 8, 2 * HD), BF16),
            pltpu.VMEM((2, CH * 8, HD), F32),
            pltpu.VMEM((2048, LAT), BF16),
            pltpu.VMEM((LAT, 2 * HD), BF16),
            pltpu.VMEM((2048, 256), BF16),
            pltpu.VMEM((16, 2, CH, LAT), BF16),
            pltpu.VMEM((4, NEW, 8, HD), BF16),
            pltpu.VMEM((NEW * 8, HD), F32),
            pltpu.VMEM((HD, COLS), BF16),
            pltpu.VMEM((1, COLS), F32),
            pltpu.VMEM((1, COLS), F32),
            pltpu.VMEM((HD, COLS), F32),
            pltpu.VMEM((4, HD + 16, 128), BF16),
            pltpu.VMEM((3, HD + 16, 128), BF16),
            pltpu.VMEM((HD + 16, 128), BF16),
            pltpu.VMEM((3, HD + 16, 128), BF16),
            pltpu.VMEM((2, 4, 2 * NEW, HD), BF16),
            pltpu.VMEM((4, NEW, 256), BF16),
            pltpu.VMEM((4, NEW, 256), BF16),
            dma(NCH), dma(4), dma(12), dma(16), dma(16), dma(16), dma(6), dma(6),
            dma(3), dma(3), dma(3), dma(3), dma(8), dma(8), dma(3), dma(3), dma(3), dma(3),
            pltpu.SemaphoreType.REGULAR((3,)),
        ],
        compiler_params=pltpu.CompilerParams(
            collective_id=0, has_side_effects=True, vmem_limit_bytes=63 * 1024 * 1024),
        cost_estimate=pl.CostEstimate(flops=3_000_000_000, bytes_accessed=7_000_000, transcendentals=1_600_000),
    )(key_value_rows[0], queries[0], w_comp, latent_gain, w_up, w_out, replica_order)


def solution(mesh):
    placed = (
        P("rep", ("seq", "tensor"), None, None),
        P("rep", None, "tensor", None),
        P(),
        P(),
        P("tensor", None, None),
        P("tensor", "seq"),
        P(),
    )
    return jax.shard_map(
        shards, mesh=mesh, in_specs=placed, out_specs=P("rep", None, "seq"), check_vma=False
    )
```
